512 devices in a mesh: ctx: 64 (over y, z), tp: 8 (over x, core).
Axes of the slice: x: 4, y: 4, z: 16, core: 2. Of those that a mesh axis runs over, the one named last changes fastest.
Arguments:
- queries: bfloat16 [8192, 16384], P('ctx', 'tp'), may hold values from -16 to 16
- keys: bfloat16 [8192, 1024], P('ctx', 'tp'), may hold values from -16 to 16
- values: bfloat16 [8192, 1024], P('ctx', 'tp'), may hold values from -6 to 6
- grad_out: bfloat16 [8192, 16384], P('ctx', 'tp'), may hold values from -6 to 6
- doc_lengths: int32 [32], replicated, may hold values from 1 to 512, 8192 in all
Outputs:
- grad_q: bfloat16 [8192, 16384], P('ctx', 'tp')
- grad_k: bfloat16 [8192, 1024], P('ctx', 'tp')
- grad_v: bfloat16 [8192, 1024], P('ctx', 'tp')
The draws below stay inside these ranges and needn't reach their ends.
Inputs may be any that keep to these rules, and one draw needn't show every extreme that they name: `doc_lengths`: 32 lengths that sum to 8192; the longest is exactly 512.
All inputs are finite; a program needn't handle non-finite values.
Results may differ from the reference program's by a relative error of at most 0.035.
Values may be sent and summed in bfloat16 or wider, within the bound.
No kernel may reach another device: no remote copies, remote signals or barrier semaphores. Data moves between devices by JAX's collectives and lax.ppermute only.
A program may use at most 64 MiB of HBM per device.

```python
import math
import jax
import jax.numpy as jnp
import numpy as np
from jax import lax

HEADS = 128
KV_HEADS = 8
HEAD_DIM = 128
TOK_DEV = 128
REACH = 4
TOKENS = 8192
MOST = 512
DOCS = 32


def shared_base(key):
    return jnp.clip(jax.random.normal(key, (TOKENS, KV_HEADS, HEAD_DIM), jnp.float32), -3.0, 3.0)


def draw_keys(key, part):
    base = shared_base(key)
    result = base
    return result.reshape(TOKENS, KV_HEADS * HEAD_DIM).astype(jnp.bfloat16)


def draw_queries(key, part):
    key = jax.random.fold_in(key, 23)
    first = jax.random.fold_in(key, 0)
    group = HEADS // KV_HEADS
    noise = jnp.clip(jax.random.normal(first, (TOKENS, KV_HEADS, group, HEAD_DIM), jnp.float32), -3.0, 3.0)
    result = noise * 2.0
    return result.reshape(TOKENS, HEADS * HEAD_DIM).astype(jnp.bfloat16)


def level_of(rng, shape, pieces, least, high):
    gain = 1.0
    for axis_at, blocks in pieces:
        heights = jax.random.uniform(jax.random.fold_in(jax.random.fold_in(rng, 6), axis_at), (blocks,), jnp.float32, least / len(pieces), high / len(pieces))
        gain = gain * jnp.repeat(jnp.exp(heights), shape[axis_at] // blocks).reshape((-1,) + (1,) * (len(shape) - 1 - axis_at))
    return gain


def split_up(number_of, total, reach, slope):
    weights = [(1 << 20) // math.isqrt(standing ** slope) + 1 for standing in range(2, number_of + 1)]
    surplus, given = total - reach - (number_of - 1), [1] * (number_of - 1)
    while surplus > 0:
        candidates = [i for i in range(number_of - 1) if given[i] < reach]
        pool, left = sum([weights[i] for i in candidates]), surplus
        for i in candidates:
            addition = min(reach - given[i], max(1, left * weights[i] // pool), surplus)
            given[i] = given[i] + addition
            surplus = surplus - addition
    return np.array([reach] + given)


def uneven(rng, count, total, limit, skew):
    if count == 2:
        one = jax.random.randint(rng, (), max(1, total - limit), min(limit, total - 1) + 1)
        return jnp.stack([one, total - one])
    tallies = jnp.asarray(split_up(count, total, limit, skew), jnp.int32)
    pairs = (count - 1) // 2
    source_of, sink = tallies[1:1 + 2 * pairs:2], tallies[2:2 + 2 * pairs:2]
    slack = jnp.minimum(source_of - 1, limit - sink)
    passed = jax.random.randint(jax.random.fold_in(rng, 1), (pairs,), 0, 1 << 20) % (slack + 1)
    tallies = tallies.at[1:1 + 2 * pairs:2].set(source_of - passed).at[2:2 + 2 * pairs:2].set(sink + passed)
    return tallies[jax.random.permutation(jax.random.fold_in(rng, 2), count)]


def centred(own_key, dims, scale, reach, shards=(), kind=jnp.bfloat16):
    values = jax.random.normal(own_key, dims, jnp.float32) * scale
    if len(shards) > 0:
        values = level_of(own_key, dims, shards, -0.22, 0.18) * values
    return jnp.clip(values, min=-reach, max=reach).astype(kind)


def setup_inputs(seed: int = 0) -> dict:
    arg_keys = jax.random.split(jax.random.key(seed), 6)
    return {
        "queries": draw_queries(jax.random.fold_in(arg_keys[5], 71), 0),
        "keys": draw_keys(jax.random.fold_in(arg_keys[5], 71), 0),
        "values": centred(arg_keys[2], (TOKENS, KV_HEADS * HEAD_DIM), 1.0, 6.0, ((0, 64), (1, 8))),
        "grad_out": centred(arg_keys[3], (TOKENS, HEADS * HEAD_DIM), 1.0, 6.0, ((0, 64), (1, 8))),
        "doc_lengths": uneven(arg_keys[4], DOCS, TOKENS, MOST, 2).astype(jnp.int32),
    }


def segment_of(positions, ends):
    return lax.optimization_barrier(jnp.sum((positions[:, None] >= ends[None, :]).astype(jnp.int32), axis=1))

def make_mask(query_pos, key_pos, ends):
    query_seg = segment_of(query_pos, ends)
    key_seg = segment_of(key_pos, ends)
    visible = (key_pos[None, :] <= query_pos[:, None]) & (key_pos[None, :] >= 0)
    visible = visible & (key_seg[None, :] == query_seg[:, None])
    return visible[None, None, :, :]

def attend(query_blk, key_win, value_win, grad_blk, mask):
    scale = 1.0 / jnp.sqrt(jnp.float32(key_win.shape[-1]))
    qf = query_blk.astype(jnp.float32)
    kf = key_win.astype(jnp.float32)
    vf = value_win.astype(jnp.float32)
    gf = grad_blk.astype(jnp.float32)
    scores = jnp.einsum('qghd,kgd->ghqk', qf, kf) * scale
    scores = jnp.where(mask, scores, -1e+30)
    peak = lax.optimization_barrier(jnp.max(scores, axis=-1, keepdims=True))
    total = lax.optimization_barrier(jnp.sum(jnp.where(mask, jnp.exp(scores - peak), 0.0), axis=-1, keepdims=True))
    lse = peak + jnp.log(total)
    probs = jnp.where(mask, jnp.exp(scores - lse), 0.0)
    probs_b = probs.astype(jnp.bfloat16)
    pf = probs_b.astype(jnp.float32)
    output = jnp.einsum('ghqk,kgd->qghd', pf, vf).astype(jnp.bfloat16)
    delta = jnp.einsum('qghd,qghd->ghq', gf, output.astype(jnp.float32))
    dprobs = jnp.einsum('qghd,kgd->ghqk', gf, vf)
    dscore = (probs * (dprobs - delta[..., None])).astype(jnp.bfloat16)
    df = dscore.astype(jnp.float32)
    grad_query = (jnp.einsum('ghqk,kgd->qghd', df, kf) * scale).astype(jnp.bfloat16)
    grad_key = jnp.einsum('ghqk,qghd->kgd', df, qf) * scale
    grad_value = jnp.einsum('ghqk,qghd->kgd', pf, gf)
    return (grad_query, grad_key, grad_value)

def reference(queries, keys, values, grad_out, doc_lengths):
    block = REACH * TOK_DEV
    group = HEADS // KV_HEADS
    nblocks = TOKENS // block
    ends = jnp.cumsum(doc_lengths).astype(jnp.int32)
    query4 = queries.reshape(TOKENS, KV_HEADS, group, HEAD_DIM)
    grad4 = grad_out.reshape(TOKENS, KV_HEADS, group, HEAD_DIM)
    padding = jnp.zeros((block, KV_HEADS, HEAD_DIM), jnp.bfloat16)
    key_pad = jnp.concatenate([padding, keys.reshape(TOKENS, KV_HEADS, HEAD_DIM)], axis=0)
    value_pad = jnp.concatenate([padding, values.reshape(TOKENS, KV_HEADS, HEAD_DIM)], axis=0)

    def one_head(head):
        head = head.astype(jnp.int32)
        query_g = lax.dynamic_slice_in_dim(query4, head, 1, 1)
        grad_g = lax.dynamic_slice_in_dim(grad4, head, 1, 1)
        key_g = lax.dynamic_slice_in_dim(key_pad, head, 1, 1)
        value_g = lax.dynamic_slice_in_dim(value_pad, head, 1, 1)

        def step(carry, index):
            start = (index * block).astype(jnp.int32)
            query_blk = lax.dynamic_slice_in_dim(query_g, start, block, 0)
            grad_blk = lax.dynamic_slice_in_dim(grad_g, start, block, 0)
            key_win = lax.dynamic_slice_in_dim(key_g, start, 2 * block, 0)
            value_win = lax.dynamic_slice_in_dim(value_g, start, 2 * block, 0)
            query_pos = start + jnp.arange(block, dtype=jnp.int32)
            key_pos = start - block + jnp.arange(2 * block, dtype=jnp.int32)
            mask = make_mask(query_pos, key_pos, ends)
            grad_query, grad_key, grad_value = attend(query_blk, key_win, value_win, grad_blk, mask)
            key_acc, value_acc = carry
            key_acc = lax.dynamic_update_slice_in_dim(key_acc, lax.dynamic_slice_in_dim(key_acc, start, 2 * block, 0) + grad_key, start, 0)
            value_acc = lax.dynamic_update_slice_in_dim(value_acc, lax.dynamic_slice_in_dim(value_acc, start, 2 * block, 0) + grad_value, start, 0)
            return ((key_acc, value_acc), grad_query)
        zeros = jnp.zeros((TOKENS + block, 1, HEAD_DIM), jnp.float32)
        (key_acc, value_acc), grad_queries = lax.scan(step, (zeros, zeros), jnp.arange(nblocks, dtype=jnp.int32))
        return (grad_queries.reshape(TOKENS, group, HEAD_DIM), key_acc[block:, 0], value_acc[block:, 0])
    grad_qs, grad_ks, grad_vs = lax.map(one_head, jnp.arange(KV_HEADS, dtype=jnp.int32))
    grad_q = jnp.transpose(grad_qs, (1, 0, 2, 3)).reshape(TOKENS, HEADS * HEAD_DIM)
    grad_k = jnp.transpose(grad_ks, (1, 0, 2)).reshape(TOKENS, KV_HEADS * HEAD_DIM).astype(jnp.bfloat16)
    grad_v = jnp.transpose(grad_vs, (1, 0, 2)).reshape(TOKENS, KV_HEADS * HEAD_DIM).astype(jnp.bfloat16)
    return (grad_q, grad_k, grad_v)
```

```python
import math

import jax
import jax.numpy as jnp
from jax import lax
from jax.experimental import pallas as pl
from jax.experimental.pallas import tpu as pltpu
from jax.sharding import PartitionSpec as P

HEADS = 128
KV_HEADS = 8
HEAD_DIM = 128
REACH = 4
TOK = 128
GROUP = HEADS // KV_HEADS
PAIR = 2
WIDE = PAIR * TOK
DOCS = 32
F32 = jnp.float32
BF16 = jnp.bfloat16
NT = (((1,), (1,)), ((), ()))
NN = (((1,), (0,)), ((), ()))


def dot(a, b, dims):
    return lax.dot_general(a, b, dims, preferred_element_type=F32)


def doc_starts(lengths_ref, row):
    total = jnp.int32(0)
    starts = jnp.zeros_like(row)
    for doc in range(DOCS):
        total = total + lengths_ref[doc]
        starts = jnp.where(total <= row, total, starts)
    return starts


def attend_kernel(
    index_ref,
    lengths_ref,
    query_ref,
    grad_ref,
    own_ref,
    one_ref,
    two_ref,
    three_ref,
    four_ref,
    grad_query_ref,
    own_out_ref,
    one_out_ref,
    two_out_ref,
    three_out_ref,
    four_out_ref,
    key_ref,
    key_t_ref,
    value_ref,
    bias_ref,
    key_acc_ref,
    value_acc_ref,
):
    scale = 1.0 / math.sqrt(HEAD_DIM)
    window = (three_ref, two_ref, one_ref, own_ref, four_ref)
    for at, block in enumerate(window):
        rows = slice(at * TOK, (at + 1) * TOK)
        key_ref[rows, :] = block[:, :HEAD_DIM]
        value_ref[rows, :] = block[:, HEAD_DIM:]
    key_t_ref[...] = key_ref[...].T

    first = index_ref[0] * TOK
    query_pos = first + lax.broadcasted_iota(jnp.int32, (1, TOK), 1)
    starts = doc_starts(lengths_ref, query_pos)
    lane = lax.broadcasted_iota(jnp.int32, (TOK, TOK), 1)
    row = lax.broadcasted_iota(jnp.int32, (TOK, TOK), 0)
    own_side = row <= lane
    for at, back in enumerate((3, 2, 1, 0)):
        key_pos = first - back * TOK + row
        if back == 0:
            key_pos = jnp.where(own_side, key_pos, key_pos - REACH * TOK)
        bias_ref[at * TOK : (at + 1) * TOK, :] = jnp.where(key_pos >= starts, 0.0, -1e30)
    own_wide = jnp.concatenate([own_side] * PAIR, axis=1)
    split = 3 * TOK

    key_acc_ref[...] = jnp.zeros_like(key_acc_ref)
    value_acc_ref[...] = jnp.zeros_like(value_acc_ref)

    def merged(scores):
        own = jnp.where(own_wide, scores[split : split + TOK], scores[split + TOK :])
        return jnp.concatenate([scores[:split], own], axis=0)

    def parted(blocks):
        own = blocks[split:]
        zero = jnp.zeros_like(own)
        return jnp.concatenate(
            [blocks[:split], jnp.where(own_wide, own, zero), jnp.where(own_wide, zero, own)], axis=0
        )

    def turn(step):
        heads = [pl.ds(pl.multiple_of((step * PAIR + h) * HEAD_DIM, HEAD_DIM), HEAD_DIM) for h in range(PAIR)]
        query = jnp.concatenate([query_ref[:, head] for head in heads], axis=0)
        grad = jnp.concatenate([grad_ref[:, head] for head in heads], axis=0)
        bias = jnp.concatenate([bias_ref[...]] * PAIR, axis=1)
        scores = merged(dot(key_ref[...], query, NT)) * (scale * math.log2(math.e)) + bias
        dprobs = merged(dot(value_ref[...], grad, NT))
        peak = jnp.max(scores, axis=0, keepdims=True)
        weights = jnp.exp2(scores - peak)
        inverse = 1.0 / jnp.sum(weights, axis=0, keepdims=True)
        delta = jnp.sum(weights * dprobs, axis=0, keepdims=True) * inverse
        probs = weights * inverse
        dscore = parted(probs * (dprobs - delta)).astype(BF16)
        probs = parted(probs).astype(BF16)
        value_acc_ref[...] += dot(probs, grad, NN)
        key_acc_ref[...] += dot(dscore, query, NN)
        grad_query = (dot(key_t_ref[...], dscore, NN) * scale).T.astype(BF16)
        for h, head in enumerate(heads):
            grad_query_ref[:, head] = grad_query[h * TOK : (h + 1) * TOK]

    for step in range(GROUP // PAIR):
        turn(step)

    outs = (three_out_ref, two_out_ref, one_out_ref, own_out_ref, four_out_ref)
    for at, out in enumerate(outs):
        rows = slice(at * TOK, (at + 1) * TOK)
        out[:, :HEAD_DIM] = (key_acc_ref[rows, :] * scale).astype(out.dtype)
        out[:, HEAD_DIM:] = value_acc_ref[rows, :].astype(out.dtype)


def attend(index, lengths, queries, grad_out, blocks):
    whole = pl.BlockSpec(memory_space=pltpu.VMEM)
    scalars = pl.BlockSpec(memory_space=pltpu.SMEM)
    both = (TOK, 2 * HEAD_DIM)
    width = (REACH + 1) * TOK
    return pl.pallas_call(
        attend_kernel,
        out_shape=(
            jax.ShapeDtypeStruct(queries.shape, BF16),
            jax.ShapeDtypeStruct(both, F32),
            *(jax.ShapeDtypeStruct(both, BF16) for _ in range(REACH)),
        ),
        in_specs=[scalars] * 2 + [whole] * (3 + REACH),
        out_specs=[whole] * (2 + REACH),
        scratch_shapes=[
            pltpu.VMEM((width, HEAD_DIM), BF16),
            pltpu.VMEM((HEAD_DIM, width), BF16),
            pltpu.VMEM((width, HEAD_DIM), BF16),
            pltpu.VMEM((REACH * TOK, TOK), F32),
            pltpu.VMEM((width, HEAD_DIM), F32),
            pltpu.VMEM((width, HEAD_DIM), F32),
        ],
        compiler_params=pltpu.CompilerParams(vmem_limit_bytes=32 * 1024 * 1024),
        cost_estimate=pl.CostEstimate(flops=2 * 10**9, bytes_accessed=2 * 10**6, transcendentals=10**6),
        name="attend",
    )(index, lengths, queries, grad_out, *blocks)


def passed_along(array, by):
    devices = lax.axis_size("ctx")
    pairs = [(i, i + by) for i in range(devices) if 0 <= i + by < devices]
    return lax.ppermute(array, "ctx", pairs)


def local(queries, keys, values, grad_out, doc_lengths):
    index = lax.axis_index("ctx").astype(jnp.int32).reshape(1)
    own = jnp.concatenate([keys, values], axis=1)
    blocks = [own] + [passed_along(own, by) for by in range(1, REACH + 1)]
    grad_q, mine, *shares = attend(index, doc_lengths, queries, grad_out, blocks)
    total = mine
    for by, share in enumerate(shares, 1):
        total = total + passed_along(share, -by).astype(F32)
    total = total.astype(BF16)
    return (grad_q, total[:, :HEAD_DIM], total[:, HEAD_DIM:])


def solution(mesh):
    placed = (P("ctx", "tp"), P("ctx", "tp"), P("ctx", "tp"), P("ctx", "tp"), P())
    return jax.shard_map(
        local,
        mesh=mesh,
        in_specs=placed,
        out_specs=(P("ctx", "tp"), P("ctx", "tp"), P("ctx", "tp")),
        check_vma=False,
    )
```

```python
import math

import jax
import jax.numpy as jnp
from jax import lax
from jax.experimental import pallas as pl
from jax.experimental.pallas import tpu as pltpu
from jax.sharding import PartitionSpec as P

HEADS = 128
KV_HEADS = 8
HEAD_DIM = 128
REACH = 4
TOK = 128
GROUP = HEADS // KV_HEADS
ROWS = GROUP * TOK
PAIR = 2
WIDE = PAIR * TOK
STEPS = GROUP // PAIR
DOCS = 32
NEAR = (1, 3)
HOP = 1
SCALE = 1.0 / math.sqrt(HEAD_DIM)
SCALE_LOG2E = SCALE * math.log2(math.e)
MASKED = -1e30
F32 = jnp.float32
BF16 = jnp.bfloat16
NT = (((1,), (1,)), ((), ()))
NN = (((1,), (0,)), ((), ()))


def dot(a, b, dims):
    return lax.dot_general(a, b, dims, preferred_element_type=F32)


def key_of(block):
    return block[:TOK]


def value_of(block):
    return block[TOK:]


def columns(step):
    return slice(step * WIDE, (step + 1) * WIDE)


def doc_starts(lengths_ref, row):
    total = jnp.int32(0)
    starts = jnp.zeros_like(row)
    for doc in range(DOCS):
        total = total + lengths_ref[doc]
        starts = jnp.where(total <= row, total, starts)
    return starts


def positions(index_ref, lengths_ref):
    first = index_ref[0] * TOK
    query_pos = first + lax.broadcasted_iota(jnp.int32, (1, TOK), 1)
    starts = doc_starts(lengths_ref, query_pos)
    key_pos = first + lax.broadcasted_iota(jnp.int32, (TOK, TOK), 0)
    return key_pos, starts


def bias_of(key_pos, starts):
    bias = jnp.where(key_pos >= starts, 0.0, MASKED)
    return jnp.concatenate([bias] * PAIR, axis=1)


def own_side():
    lane = lax.broadcasted_iota(jnp.int32, (TOK, WIDE), 1)
    row = lax.broadcasted_iota(jnp.int32, (TOK, WIDE), 0)
    return row <= lax.rem(lane, TOK)


def top(x):
    return jnp.max(x, axis=0, keepdims=True)


def total(x):
    return jnp.sum(x, axis=0, keepdims=True)


def load_kernel(
    index_ref,
    lengths_ref,
    query_hbm,
    grad_hbm,
    own_ref,
    query_ref,
    grad_ref,
    score_ref,
    dprob_ref,
    near_bias_ref,
    far_bias_ref,
    query_sems,
    grad_sems,
):
    def copies(head):
        there, here = pl.ds(head * HEAD_DIM, HEAD_DIM), pl.ds(head * TOK, TOK)
        return (
            pltpu.make_async_copy(query_hbm.at[:, there], query_ref.at[here, :], query_sems.at[head]),
            pltpu.make_async_copy(grad_hbm.at[:, there], grad_ref.at[here, :], grad_sems.at[head]),
        )

    for head in range(GROUP):
        for copy in copies(head):
            copy.start()
    key_pos, starts = positions(index_ref, lengths_ref)
    for at, back in enumerate(NEAR):
        near_bias_ref[at * TOK : (at + 1) * TOK, :] = bias_of(key_pos - back * TOK, starts)
    far_bias_ref[:TOK, :] = bias_of(key_pos - (NEAR[0] + HOP) * TOK, starts)
    far_bias_ref[TOK:, :] = jnp.where(own_side(), bias_of(key_pos, starts), bias_of(key_pos - REACH * TOK, starts))
    for step in range(STEPS):
        for head in range(step * PAIR, (step + 1) * PAIR):
            for copy in copies(head):
                copy.wait()
        at = columns(step)
        score_ref[:, at] = dot(key_of(own_ref), query_ref[at, :], NT)
        dprob_ref[:, at] = dot(value_of(own_ref), grad_ref[at, :], NT)


def near_kernel(bias_ref, query_ref, grad_ref, near_a_ref, near_b_ref, weight_ref, dprob_ref, stat_ref):
    keys = jnp.concatenate([key_of(near_a_ref), key_of(near_b_ref)], axis=0)
    values = jnp.concatenate([value_of(near_a_ref), value_of(near_b_ref)], axis=0)
    for step in range(STEPS):
        at = columns(step)
        scores = dot(keys, query_ref[at, :], NT) * SCALE_LOG2E + bias_ref[...]
        dprobs = dot(values, grad_ref[at, :], NT)
        peak = top(scores)
        weights = jnp.exp2(scores - peak)
        weight_ref[:, at] = weights
        dprob_ref[:, at] = dprobs
        stat_ref[0:1, at] = peak
        stat_ref[1:2, at] = total(weights)
        stat_ref[2:3, at] = total(weights * dprobs)


def far_kernel(
    bias_ref,
    query_ref,
    grad_ref,
    score_ref,
    dprob_ref,
    near_stat_ref,
    far_a_ref,
    far_b_ref,
    sums_ref,
    far_dscore_ref,
    own_prob_ref,
    own_dscore_ref,
    stat_ref,
    far_prob_ref,
):
    own = own_side()
    keys = jnp.concatenate([key_of(far_a_ref), key_of(far_b_ref)], axis=0)
    values = jnp.concatenate([value_of(far_a_ref), value_of(far_b_ref)], axis=0)

    def joined(fresh, mine):
        return jnp.concatenate([fresh[:TOK], jnp.where(own, mine, fresh[TOK:])], axis=0)

    for step in range(STEPS):
        at = columns(step)
        scores = joined(dot(keys, query_ref[at, :], NT), score_ref[:, at]) * SCALE_LOG2E + bias_ref[...]
        dprobs = joined(dot(values, grad_ref[at, :], NT), dprob_ref[:, at])
        near_peak = near_stat_ref[0:1, at]
        peak = jnp.maximum(top(scores), near_peak)
        weights = jnp.exp2(scores - peak)
        near_factor = jnp.exp2(near_peak - peak)
        inverse = 1.0 / (total(weights) + near_stat_ref[1:2, at] * near_factor)
        delta = (total(weights * dprobs) + near_stat_ref[2:3, at] * near_factor) * inverse
        stat_ref[0:1, at] = near_factor * inverse
        stat_ref[1:2, at] = delta
        probs = weights * inverse
        dscores = probs * (dprobs - delta)
        far_prob_ref[:TOK, at] = probs[:TOK].astype(BF16)
        far_dscore_ref[:TOK, at] = dscores[:TOK].astype(BF16)
        far_prob_ref[TOK:, at] = jnp.where(own, 0.0, probs[TOK:]).astype(BF16)
        far_dscore_ref[TOK:, at] = jnp.where(own, 0.0, dscores[TOK:]).astype(BF16)
        own_prob_ref[:, at] = jnp.where(own, probs[TOK:], 0.0).astype(BF16)
        own_dscore_ref[:, at] = jnp.where(own, dscores[TOK:], 0.0).astype(BF16)
    keys = (dot(far_dscore_ref[...], query_ref[...], NN) * SCALE).astype(BF16)
    values = dot(far_prob_ref[...], grad_ref[...], NN).astype(BF16)
    for at in range(len(NEAR)):
        rows = slice(at * TOK, (at + 1) * TOK)
        sums_ref[2 * at * TOK : (2 * at + 1) * TOK] = keys[rows]
        sums_ref[(2 * at + 1) * TOK : (2 * at + 2) * TOK] = values[rows]


def rest_kernel(
    query_ref,
    grad_ref,
    weight_ref,
    dprob_ref,
    stat_ref,
    far_dscore_ref,
    own_prob_ref,
    own_dscore_ref,
    own_ref,
    near_a_ref,
    far_a_ref,
    near_b_ref,
    far_b_ref,
    grad_query_hbm,
    own_sums_ref,
    near_a_sums_ref,
    near_b_sums_ref,
    near_prob_ref,
    near_dscore_ref,
    grad_query_ref,
    out_sems,
):
    far_keys = jnp.concatenate([key_of(far_a_ref), key_of(far_b_ref)], axis=0).T
    near_keys = jnp.concatenate([key_of(near_a_ref), key_of(near_b_ref)], axis=0).T
    own_keys = key_of(own_ref).T

    def out_copy(step):
        at = pl.ds(step * WIDE, WIDE)
        return pltpu.make_async_copy(grad_query_ref.at[:, at], grad_query_hbm.at[:, at], out_sems.at[step])

    for step in range(STEPS):
        at = columns(step)
        probs = weight_ref[:, at] * stat_ref[0:1, at]
        dscores = (probs * (dprob_ref[:, at] - stat_ref[1:2, at])).astype(BF16)
        near_prob_ref[:, at] = probs.astype(BF16)
        near_dscore_ref[:, at] = dscores
        grad_query = dot(far_keys, far_dscore_ref[:, at], NN) + dot(near_keys, dscores, NN)
        grad_query = ((grad_query + dot(own_keys, own_dscore_ref[:, at], NN)) * SCALE).T.astype(BF16)
        for h in range(PAIR):
            head = slice((step * PAIR + h) * HEAD_DIM, (step * PAIR + h + 1) * HEAD_DIM)
            grad_query_ref[:, head] = grad_query[h * TOK : (h + 1) * TOK]
        out_copy(step).start()
    near_keys = dot(near_dscore_ref[...], query_ref[...], NN) * SCALE
    near_values = dot(near_prob_ref[...], grad_ref[...], NN)
    for at, sums_ref in enumerate((near_a_sums_ref, near_b_sums_ref)):
        rows = slice(at * TOK, (at + 1) * TOK)
        sums_ref[:TOK] = near_keys[rows]
        sums_ref[TOK:] = near_values[rows]
    own_sums_ref[:TOK] = dot(own_dscore_ref[...], query_ref[...], NN) * SCALE
    own_sums_ref[TOK:] = dot(own_prob_ref[...], grad_ref[...], NN)
    for step in range(STEPS):
        out_copy(step).wait()


WHOLE = pl.BlockSpec(memory_space=pltpu.VMEM)
SCALARS = pl.BlockSpec(memory_space=pltpu.SMEM)
FAR = pl.BlockSpec(memory_space=pl.ANY)


def call(kernel, name, flops, in_specs, outs, scratch, *args, traffic=10**6):
    return pl.pallas_call(
        kernel,
        out_shape=[jax.ShapeDtypeStruct(shape, dtype) for shape, dtype, _ in outs],
        in_specs=in_specs,
        out_specs=[spec for _, _, spec in outs],
        scratch_shapes=scratch,
        compiler_params=pltpu.CompilerParams(vmem_limit_bytes=16 * 1024 * 1024),
        cost_estimate=pl.CostEstimate(flops=flops, bytes_accessed=traffic, transcendentals=10**5),
        name=name,
    )(*args)


def load(index, lengths, queries, grad_out, own):
    return call(
        load_kernel,
        "load",
        2 * 10**8,
        [SCALARS] * 2 + [FAR, FAR, WHOLE],
        [((ROWS, HEAD_DIM), BF16, WHOLE)] * 2
        + [((TOK, ROWS), F32, WHOLE)] * 2
        + [((2 * TOK, WIDE), F32, WHOLE)] * 2,
        [pltpu.SemaphoreType.DMA((GROUP,))] * 2,
        index,
        lengths,
        queries,
        grad_out,
        own,
        traffic=0,
    )


def near_part(bias, query, grad, near_a, near_b):
    return call(
        near_kernel,
        "near_part",
        4 * 10**8,
        [WHOLE] * 5,
        [((2 * TOK, ROWS), F32, WHOLE)] * 2 + [((8, ROWS), F32, WHOLE)],
        [],
        bias,
        query,
        grad,
        near_a,
        near_b,
    )


def far_part(bias, query, grad, score, dprob, near_stat, far_a, far_b):
    return call(
        far_kernel,
        "far_part",
        6 * 10**8,
        [WHOLE] * 8,
        [
            ((4 * TOK, HEAD_DIM), BF16, WHOLE),
            ((2 * TOK, ROWS), BF16, WHOLE),
            ((TOK, ROWS), BF16, WHOLE),
            ((TOK, ROWS), BF16, WHOLE),
            ((8, ROWS), F32, WHOLE),
        ],
        [pltpu.VMEM((2 * TOK, ROWS), BF16)],
        bias,
        query,
        grad,
        score,
        dprob,
        near_stat,
        far_a,
        far_b,
    )


def rest_part(query, grad, weight, dprob, stat, far_dscore, own_prob, own_dscore, *blocks):
    return call(
        rest_kernel,
        "rest_part",
        8 * 10**8,
        [WHOLE] * 13,
        [
            ((TOK, GROUP * HEAD_DIM), BF16, FAR),
            *[((2 * TOK, HEAD_DIM), F32, WHOLE)] * 3,
        ],
        [
            pltpu.VMEM((2 * TOK, ROWS), BF16),
            pltpu.VMEM((2 * TOK, ROWS), BF16),
            pltpu.VMEM((TOK, GROUP * HEAD_DIM), BF16),
            pltpu.SemaphoreType.DMA((STEPS,)),
        ],
        query,
        grad,
        weight,
        dprob,
        stat,
        far_dscore,
        own_prob,
        own_dscore,
        *blocks,
    )


def passed_along(array, by):
    devices = lax.axis_size("ctx")
    pairs = [(i, i + by) for i in range(devices) if 0 <= i + by < devices]
    return lax.ppermute(array, "ctx", pairs)


def local(queries, keys, values, grad_out, doc_lengths):
    index = lax.axis_index("ctx").astype(jnp.int32).reshape(1)
    low = jnp.array(-jnp.inf, BF16)
    own = lax.max(
        lax.pad(keys, low, ((0, TOK, 0), (0, 0, 0))), lax.pad(values, low, ((TOK, 0, 0), (0, 0, 0)))
    )
    near_b = passed_along(own, NEAR[1])
    near_a = passed_along(own, NEAR[0])
    query, grad, own_score, own_dprob, near_bias, far_bias = load(index, doc_lengths, queries, grad_out, own)
    near_b, near_a, far_bias = lax.optimization_barrier((near_b, near_a, far_bias))
    far = passed_along(jnp.concatenate([near_a, near_b], axis=0), HOP)
    near_weight, near_dprob, near_stat = near_part(near_bias, query, grad, near_a, near_b)
    far_a, far_b = far[: 2 * TOK], far[2 * TOK :]
    far_sums, far_dscore, own_prob, own_dscore, stat = far_part(
        far_bias, query, grad, own_score, own_dprob, near_stat, far_a, far_b
    )
    far_sums = passed_along(far_sums, -HOP)
    grad_q, own_sums, near_a_sums, near_b_sums = rest_part(
        query, grad, near_weight, near_dprob, stat, far_dscore, own_prob, own_dscore, own, near_a, far_a, near_b, far_b
    )
    near_b_sums = (near_b_sums + far_sums[2 * TOK :].astype(F32)).astype(BF16)
    near_a_sums = (near_a_sums + far_sums[: 2 * TOK].astype(F32)).astype(BF16)
    near_b_sums = passed_along(near_b_sums, -NEAR[1])
    near_a_sums = passed_along(near_a_sums, -NEAR[0])
    sums = (own_sums + near_b_sums.astype(F32) + near_a_sums.astype(F32)).astype(BF16)
    return (grad_q, key_of(sums), value_of(sums))


def solution(mesh):
    placed = (P("ctx", "tp"), P("ctx", "tp"), P("ctx", "tp"), P("ctx", "tp"), P())
    return jax.shard_map(
        local,
        mesh=mesh,
        in_specs=placed,
        out_specs=(P("ctx", "tp"), P("ctx", "tp"), P("ctx", "tp")),
        check_vma=False,
    )
```

```python
import math

import jax
import jax.numpy as jnp
from jax import lax
from jax.experimental import pallas as pl
from jax.experimental.pallas import tpu as pltpu
from jax.sharding import PartitionSpec as P

HEADS = 128
KV_HEADS = 8
HEAD_DIM = 128
REACH = 4
TOK = 128
GROUP = HEADS // KV_HEADS
ROWS = GROUP * TOK
PAIR = 2
WIDE = PAIR * TOK
STEPS = GROUP // PAIR
DOCS = 32
NEAR = (1, 3)
HOP = 1
SCALE = 1.0 / math.sqrt(HEAD_DIM)
SCALE_LOG2E = SCALE * math.log2(math.e)
MASKED = -1e30
F32 = jnp.float32
BF16 = jnp.bfloat16
NT = (((1,), (1,)), ((), ()))
NN = (((1,), (0,)), ((), ()))


def dot(a, b, dims):
    return lax.dot_general(a, b, dims, preferred_element_type=F32)


def key_of(block):
    return block[:TOK]


def value_of(block):
    return block[TOK:]


def columns(step):
    return slice(step * WIDE, (step + 1) * WIDE)


def doc_starts(lengths_ref, row):
    total = jnp.int32(0)
    starts = jnp.zeros_like(row)
    for doc in range(DOCS):
        total = total + lengths_ref[doc]
        starts = jnp.where(total <= row, total, starts)
    return starts


def positions(index_ref, lengths_ref):
    first = index_ref[0] * TOK
    query_pos = first + lax.broadcasted_iota(jnp.int32, (1, TOK), 1)
    starts = doc_starts(lengths_ref, query_pos)
    key_pos = first + lax.broadcasted_iota(jnp.int32, (TOK, TOK), 0)
    return key_pos, starts


def bias_of(key_pos, starts):
    bias = jnp.where(key_pos >= starts, 0.0, MASKED)
    return jnp.concatenate([bias] * PAIR, axis=1)


def own_side():
    lane = lax.broadcasted_iota(jnp.int32, (TOK, WIDE), 1)
    row = lax.broadcasted_iota(jnp.int32, (TOK, WIDE), 0)
    return row <= lax.rem(lane, TOK)


def top(x):
    return jnp.max(x, axis=0, keepdims=True)


def total(x):
    return jnp.sum(x, axis=0, keepdims=True)


def load_kernel(
    index_ref,
    lengths_ref,
    all_query_ref,
    all_grad_ref,
    own_ref,
    query_ref,
    grad_ref,
    score_ref,
    dprob_ref,
    near_bias_ref,
    far_bias_ref,
):
    key_pos, starts = positions(index_ref, lengths_ref)
    for at, back in enumerate(NEAR):
        near_bias_ref[at * TOK : (at + 1) * TOK, :] = bias_of(key_pos - back * TOK, starts)
    far_bias_ref[:TOK, :] = bias_of(key_pos - (NEAR[0] + HOP) * TOK, starts)
    far_bias_ref[TOK:, :] = jnp.where(own_side(), bias_of(key_pos, starts), bias_of(key_pos - REACH * TOK, starts))
    for step in range(STEPS):
        for head in range(step * PAIR, (step + 1) * PAIR):
            there, here = slice(head * HEAD_DIM, (head + 1) * HEAD_DIM), slice(head * TOK, (head + 1) * TOK)
            query_ref[here, :] = all_query_ref[:, there]
            grad_ref[here, :] = all_grad_ref[:, there]
        at = columns(step)
        score_ref[:, at] = dot(key_of(own_ref), query_ref[at, :], NT)
        dprob_ref[:, at] = dot(value_of(own_ref), grad_ref[at, :], NT)


def near_kernel(bias_ref, query_ref, grad_ref, near_a_ref, near_b_ref, weight_ref, dprob_ref, stat_ref):
    keys = jnp.concatenate([key_of(near_a_ref), key_of(near_b_ref)], axis=0)
    values = jnp.concatenate([value_of(near_a_ref), value_of(near_b_ref)], axis=0)
    for step in range(STEPS):
        at = columns(step)
        scores = dot(keys, query_ref[at, :], NT) * SCALE_LOG2E + bias_ref[...]
        dprobs = dot(values, grad_ref[at, :], NT)
        peak = top(scores)
        weights = jnp.exp2(scores - peak)
        weight_ref[:, at] = weights
        dprob_ref[:, at] = dprobs
        stat_ref[0:1, at] = peak
        stat_ref[1:2, at] = total(weights)
        stat_ref[2:3, at] = total(weights * dprobs)


def far_kernel(
    bias_ref,
    query_ref,
    grad_ref,
    score_ref,
    dprob_ref,
    near_stat_ref,
    far_a_ref,
    far_b_ref,
    sums_ref,
    far_dscore_ref,
    own_prob_ref,
    own_dscore_ref,
    stat_ref,
    far_prob_ref,
):
    own = own_side()
    keys = jnp.concatenate([key_of(far_a_ref), key_of(far_b_ref)], axis=0)
    values = jnp.concatenate([value_of(far_a_ref), value_of(far_b_ref)], axis=0)

    halves = (slice(0, TOK), slice(TOK, 2 * TOK))
    for step in range(STEPS):
        at = columns(step)
        fresh_scores = dot(keys, query_ref[at, :], NT)
        fresh_dprobs = dot(values, grad_ref[at, :], NT)
        peaks, weights, dprobs, totals, products = [], [], [], [], []
        for rows in halves:
            scores, dprob = fresh_scores[rows], fresh_dprobs[rows]
            if rows.start:
                scores, dprob = jnp.where(own, score_ref[:, at], scores), jnp.where(own, dprob_ref[:, at], dprob)
            scores = scores * SCALE_LOG2E + bias_ref[rows, :]
            peak = top(scores)
            weight = jnp.exp2(scores - peak)
            peaks.append(peak)
            weights.append(weight)
            dprobs.append(dprob)
            totals.append(total(weight))
            products.append(total(weight * dprob))
        near_peak = near_stat_ref[0:1, at]
        peak = jnp.maximum(jnp.maximum(peaks[0], peaks[1]), near_peak)
        near_factor = jnp.exp2(near_peak - peak)
        factors = [jnp.exp2(part - peak) for part in peaks]
        inverse = 1.0 / (totals[0] * factors[0] + totals[1] * factors[1] + near_stat_ref[1:2, at] * near_factor)
        delta = products[0] * factors[0] + products[1] * factors[1] + near_stat_ref[2:3, at] * near_factor
        delta = delta * inverse
        stat_ref[0:1, at] = near_factor * inverse
        stat_ref[1:2, at] = delta
        probs = weights[0] * (factors[0] * inverse)
        far_prob_ref[:TOK, at] = probs.astype(BF16)
        far_dscore_ref[:TOK, at] = (probs * (dprobs[0] - delta)).astype(BF16)
        probs = weights[1] * (factors[1] * inverse)
        dscores = probs * (dprobs[1] - delta)
        far_prob_ref[TOK:, at] = jnp.where(own, 0.0, probs).astype(BF16)
        far_dscore_ref[TOK:, at] = jnp.where(own, 0.0, dscores).astype(BF16)
        own_prob_ref[:, at] = jnp.where(own, probs, 0.0).astype(BF16)
        own_dscore_ref[:, at] = jnp.where(own, dscores, 0.0).astype(BF16)
    keys = (dot(far_dscore_ref[...], query_ref[...], NN) * SCALE).astype(BF16)
    values = dot(far_prob_ref[...], grad_ref[...], NN).astype(BF16)
    for at in range(len(NEAR)):
        rows = slice(at * TOK, (at + 1) * TOK)
        sums_ref[2 * at * TOK : (2 * at + 1) * TOK] = keys[rows]
        sums_ref[(2 * at + 1) * TOK : (2 * at + 2) * TOK] = values[rows]


def rest_kernel(
    query_ref,
    grad_ref,
    weight_ref,
    dprob_ref,
    stat_ref,
    far_dscore_ref,
    own_prob_ref,
    own_dscore_ref,
    own_ref,
    near_a_ref,
    far_a_ref,
    near_b_ref,
    far_b_ref,
    grad_query_hbm,
    own_sums_ref,
    near_a_sums_ref,
    near_b_sums_ref,
    near_prob_ref,
    near_dscore_ref,
    grad_query_ref,
    out_sems,
):
    far_keys = jnp.concatenate([key_of(far_a_ref), key_of(far_b_ref)], axis=0).T
    near_keys = jnp.concatenate([key_of(near_a_ref), key_of(near_b_ref)], axis=0).T
    own_keys = key_of(own_ref).T

    def out_copy(step):
        at = pl.ds(step * WIDE, WIDE)
        return pltpu.make_async_copy(grad_query_ref.at[:, at], grad_query_hbm.at[:, at], out_sems.at[step])

    for step in range(STEPS):
        at = columns(step)
        probs = weight_ref[:, at] * stat_ref[0:1, at]
        dscores = (probs * (dprob_ref[:, at] - stat_ref[1:2, at])).astype(BF16)
        near_prob_ref[:, at] = probs.astype(BF16)
        near_dscore_ref[:, at] = dscores
        grad_query = dot(far_keys, far_dscore_ref[:, at], NN) + dot(near_keys, dscores, NN)
        grad_query = ((grad_query + dot(own_keys, own_dscore_ref[:, at], NN)) * SCALE).T.astype(BF16)
        for h in range(PAIR):
            head = slice((step * PAIR + h) * HEAD_DIM, (step * PAIR + h + 1) * HEAD_DIM)
            grad_query_ref[:, head] = grad_query[h * TOK : (h + 1) * TOK]
        out_copy(step).start()
    near_keys = dot(near_dscore_ref[...], query_ref[...], NN) * SCALE
    near_values = dot(near_prob_ref[...], grad_ref[...], NN)
    for at, sums_ref in enumerate((near_a_sums_ref, near_b_sums_ref)):
        rows = slice(at * TOK, (at + 1) * TOK)
        sums_ref[:TOK] = near_keys[rows]
        sums_ref[TOK:] = near_values[rows]
    own_sums_ref[:TOK] = dot(own_dscore_ref[...], query_ref[...], NN) * SCALE
    own_sums_ref[TOK:] = dot(own_prob_ref[...], grad_ref[...], NN)
    for step in range(STEPS):
        out_copy(step).wait()


WHOLE = pl.BlockSpec(memory_space=pltpu.VMEM)
SCALARS = pl.BlockSpec(memory_space=pltpu.SMEM)
FAR = pl.BlockSpec(memory_space=pl.ANY)


def call(kernel, name, flops, in_specs, outs, scratch, *args, traffic=10**6):
    return pl.pallas_call(
        kernel,
        out_shape=[jax.ShapeDtypeStruct(shape, dtype) for shape, dtype, _ in outs],
        in_specs=in_specs,
        out_specs=[spec for _, _, spec in outs],
        scratch_shapes=scratch,
        compiler_params=pltpu.CompilerParams(vmem_limit_bytes=16 * 1024 * 1024),
        cost_estimate=pl.CostEstimate(flops=flops, bytes_accessed=traffic, transcendentals=10**5),
        name=name,
    )(*args)


def load(index, lengths, queries, grad_out, own):
    return call(
        load_kernel,
        "load",
        2 * 10**8,
        [SCALARS] * 2 + [WHOLE] * 3,
        [((ROWS, HEAD_DIM), BF16, WHOLE)] * 2
        + [((TOK, ROWS), F32, WHOLE)] * 2
        + [((2 * TOK, WIDE), F32, WHOLE)] * 2,
        [],
        index,
        lengths,
        queries,
        grad_out,
        own,
        traffic=0,
    )


def near_part(bias, query, grad, near_a, near_b):
    return call(
        near_kernel,
        "near_part",
        4 * 10**8,
        [WHOLE] * 5,
        [((2 * TOK, ROWS), F32, WHOLE)] * 2 + [((8, ROWS), F32, WHOLE)],
        [],
        bias,
        query,
        grad,
        near_a,
        near_b,
    )


def far_part(bias, query, grad, score, dprob, near_stat, far_a, far_b):
    return call(
        far_kernel,
        "far_part",
        6 * 10**8,
        [WHOLE] * 8,
        [
            ((4 * TOK, HEAD_DIM), BF16, WHOLE),
            ((2 * TOK, ROWS), BF16, WHOLE),
            ((TOK, ROWS), BF16, WHOLE),
            ((TOK, ROWS), BF16, WHOLE),
            ((8, ROWS), F32, WHOLE),
        ],
        [pltpu.VMEM((2 * TOK, ROWS), BF16)],
        bias,
        query,
        grad,
        score,
        dprob,
        near_stat,
        far_a,
        far_b,
    )


def rest_part(query, grad, weight, dprob, stat, far_dscore, own_prob, own_dscore, *blocks):
    return call(
        rest_kernel,
        "rest_part",
        8 * 10**8,
        [WHOLE] * 13,
        [
            ((TOK, GROUP * HEAD_DIM), BF16, FAR),
            *[((2 * TOK, HEAD_DIM), F32, WHOLE)] * 3,
        ],
        [
            pltpu.VMEM((2 * TOK, ROWS), BF16),
            pltpu.VMEM((2 * TOK, ROWS), BF16),
            pltpu.VMEM((TOK, GROUP * HEAD_DIM), BF16),
            pltpu.SemaphoreType.DMA((STEPS,)),
        ],
        query,
        grad,
        weight,
        dprob,
        stat,
        far_dscore,
        own_prob,
        own_dscore,
        *blocks,
    )


def passed_along(array, by):
    devices = lax.axis_size("ctx")
    pairs = [(i, i + by) for i in range(devices) if 0 <= i + by < devices]
    return lax.ppermute(array, "ctx", pairs)


def local(queries, keys, values, grad_out, doc_lengths):
    index = lax.axis_index("ctx").astype(jnp.int32).reshape(1)
    low = jnp.array(-jnp.inf, BF16)
    own = lax.max(
        lax.pad(keys, low, ((0, TOK, 0), (0, 0, 0))), lax.pad(values, low, ((TOK, 0, 0), (0, 0, 0)))
    )
    near_b = passed_along(own, NEAR[1])
    near_a = passed_along(own, NEAR[0])
    query, grad, own_score, own_dprob, near_bias, far_bias = load(index, doc_lengths, queries, grad_out, own)
    near_b, near_a, far_bias = lax.optimization_barrier((near_b, near_a, far_bias))
    far = passed_along(jnp.concatenate([near_a, near_b], axis=0), HOP)
    near_weight, near_dprob, near_stat = near_part(near_bias, query, grad, near_a, near_b)
    far_a, far_b = far[: 2 * TOK], far[2 * TOK :]
    far_sums, far_dscore, own_prob, own_dscore, stat = far_part(
        far_bias, query, grad, own_score, own_dprob, near_stat, far_a, far_b
    )
    far_sums = passed_along(far_sums, -HOP)
    grad_q, own_sums, near_a_sums, near_b_sums = rest_part(
        query, grad, near_weight, near_dprob, stat, far_dscore, own_prob, own_dscore, own, near_a, far_a, near_b, far_b
    )
    near_b_sums = (near_b_sums + far_sums[2 * TOK :].astype(F32)).astype(BF16)
    near_a_sums = (near_a_sums + far_sums[: 2 * TOK].astype(F32)).astype(BF16)
    near_b_sums = passed_along(near_b_sums, -NEAR[1])
    near_a_sums = passed_along(near_a_sums, -NEAR[0])
    sums = (own_sums + near_a_sums.astype(F32) + near_b_sums.astype(F32)).astype(BF16)
    return (grad_q, key_of(sums), value_of(sums))


def solution(mesh):
    placed = (P("ctx", "tp"), P("ctx", "tp"), P("ctx", "tp"), P("ctx", "tp"), P())
    return jax.shard_map(
        local,
        mesh=mesh,
        in_specs=placed,
        out_specs=(P("ctx", "tp"), P("ctx", "tp"), P("ctx", "tp")),
        check_vma=False,
    )
```

```python
import math

import jax
import jax.numpy as jnp
from jax import lax
from jax.experimental import pallas as pl
from jax.experimental.pallas import tpu as pltpu
from jax.sharding import PartitionSpec as P

HEADS = 128
KV_HEADS = 8
HEAD_DIM = 128
REACH = 4
TOK = 128
GROUP = HEADS // KV_HEADS
ROWS = GROUP * TOK
PAIR = 2
WIDE = PAIR * TOK
STEPS = GROUP // PAIR
DOCS = 32
SCALE = 1.0 / math.sqrt(HEAD_DIM)
SCALE_LOG2E = SCALE * math.log2(math.e)
MASKED = -1e30
F32 = jnp.float32
BF16 = jnp.bfloat16
NT = (((1,), (1,)), ((), ()))
NN = (((1,), (0,)), ((), ()))


def dot(a, b, dims):
    return lax.dot_general(a, b, dims, preferred_element_type=F32)


def key_of(block):
    return block[:TOK]


def value_of(block):
    return block[TOK:]


def columns(step):
    return slice(step * WIDE, (step + 1) * WIDE)


def doc_starts(lengths_ref, row):
    total = jnp.int32(0)
    starts = jnp.zeros_like(row)
    for doc in range(DOCS):
        total = total + lengths_ref[doc]
        starts = jnp.where(total <= row, total, starts)
    return starts


def positions(index_ref, lengths_ref):
    first = index_ref[0] * TOK
    query_pos = first + lax.broadcasted_iota(jnp.int32, (1, TOK), 1)
    starts = doc_starts(lengths_ref, query_pos)
    key_pos = first + lax.broadcasted_iota(jnp.int32, (TOK, TOK), 0)
    return key_pos, starts


def bias_of(key_pos, starts):
    bias = jnp.where(key_pos >= starts, 0.0, MASKED)
    return jnp.concatenate([bias] * PAIR, axis=1)


def top(x):
    return jnp.max(x, axis=0, keepdims=True)


def total(x):
    return jnp.sum(x, axis=0, keepdims=True)


def load_kernel(
    index_ref, lengths_ref, wide_query_ref, wide_grad_ref, query_ref, grad_ref, near_bias_ref, far_bias_ref
):
    key_pos, starts = positions(index_ref, lengths_ref)
    row = lax.broadcasted_iota(jnp.int32, (TOK, WIDE), 0)
    lane = lax.broadcasted_iota(jnp.int32, (TOK, WIDE), 1)
    near_bias_ref[:TOK, :] = bias_of(key_pos - TOK, starts)
    near_bias_ref[TOK : 2 * TOK, :] = bias_of(key_pos - 3 * TOK, starts)
    near_bias_ref[2 * TOK :, :] = jnp.where(row <= lax.rem(lane, TOK), bias_of(key_pos, starts), MASKED)
    far_bias_ref[:TOK, :] = bias_of(key_pos - 2 * TOK, starts)
    far_bias_ref[TOK:, :] = bias_of(key_pos - 4 * TOK, starts)
    for head in range(GROUP):
        there, here = slice(head * HEAD_DIM, (head + 1) * HEAD_DIM), slice(head * TOK, (head + 1) * TOK)
        query_ref[here, :] = wide_query_ref[:, there]
        grad_ref[here, :] = wide_grad_ref[:, there]


def near_kernel(bias_ref, query_ref, grad_ref, one_ref, three_ref, own_ref, weight_ref, dprob_ref, stat_ref):
    blocks = (one_ref, three_ref, own_ref)
    keys = jnp.concatenate([key_of(block) for block in blocks], axis=0)
    values = jnp.concatenate([value_of(block) for block in blocks], axis=0)
    for step in range(STEPS):
        at = columns(step)
        scores = dot(keys, query_ref[at, :], NT) * SCALE_LOG2E + bias_ref[...]
        dprobs = dot(values, grad_ref[at, :], NT)
        peak = top(scores)
        weights = jnp.exp2(scores - peak)
        weight_ref[:, at] = weights
        dprob_ref[:, at] = dprobs
        stat_ref[0:1, at] = peak
        stat_ref[1:2, at] = total(weights)
        stat_ref[2:3, at] = total(weights * dprobs)


def far_kernel(
    bias_ref, query_ref, grad_ref, near_stat_ref, two_ref, four_ref, sums_ref, dscore_ref, stat_ref, prob_ref
):
    keys = jnp.concatenate([key_of(two_ref), key_of(four_ref)], axis=0)
    values = jnp.concatenate([value_of(two_ref), value_of(four_ref)], axis=0)
    halves = (slice(0, TOK), slice(TOK, 2 * TOK))
    for step in range(STEPS):
        at = columns(step)
        fresh_scores = dot(keys, query_ref[at, :], NT)
        fresh_dprobs = dot(values, grad_ref[at, :], NT)
        peaks, weights, dprobs, totals, products = [], [], [], [], []
        for rows in halves:
            scores, dprob = fresh_scores[rows] * SCALE_LOG2E + bias_ref[rows, :], fresh_dprobs[rows]
            peak = top(scores)
            weight = jnp.exp2(scores - peak)
            peaks.append(peak)
            weights.append(weight)
            dprobs.append(dprob)
            totals.append(total(weight))
            products.append(total(weight * dprob))
        near_peak = near_stat_ref[0:1, at]
        peak = jnp.maximum(jnp.maximum(peaks[0], peaks[1]), near_peak)
        near_factor = jnp.exp2(near_peak - peak)
        factors = [jnp.exp2(part - peak) for part in peaks]
        inverse = 1.0 / (totals[0] * factors[0] + totals[1] * factors[1] + near_stat_ref[1:2, at] * near_factor)
        delta = products[0] * factors[0] + products[1] * factors[1] + near_stat_ref[2:3, at] * near_factor
        delta = delta * inverse
        stat_ref[0:1, at] = near_factor * inverse
        stat_ref[1:2, at] = delta
        for rows, weight, dprob, factor in zip(halves, weights, dprobs, factors):
            probs = weight * (factor * inverse)
            prob_ref[rows, at] = probs.astype(BF16)
            dscore_ref[rows, at] = (probs * (dprob - delta)).astype(BF16)
    keys = (dot(dscore_ref[...], query_ref[...], NN) * SCALE).astype(BF16)
    values = dot(prob_ref[...], grad_ref[...], NN).astype(BF16)
    for at, rows in enumerate(halves):
        sums_ref[2 * at * TOK : (2 * at + 1) * TOK] = keys[rows]
        sums_ref[(2 * at + 1) * TOK : (2 * at + 2) * TOK] = values[rows]


def rest_kernel(
    query_ref,
    grad_ref,
    weight_ref,
    dprob_ref,
    stat_ref,
    far_dscore_ref,
    one_ref,
    two_ref,
    three_ref,
    four_ref,
    own_ref,
    grad_query_hbm,
    one_sums_ref,
    three_sums_ref,
    own_sums_ref,
    prob_ref,
    dscore_ref,
    grad_query_ref,
    out_sems,
):
    far_keys = jnp.concatenate([key_of(two_ref), key_of(four_ref)], axis=0).T
    near_keys = jnp.concatenate([key_of(one_ref), key_of(three_ref), key_of(own_ref)], axis=0).T

    def out_copy(step):
        at = pl.ds(step * WIDE, WIDE)
        return pltpu.make_async_copy(grad_query_ref.at[:, at], grad_query_hbm.at[:, at], out_sems.at[step])

    for step in range(STEPS):
        at = columns(step)
        probs = weight_ref[:, at] * stat_ref[0:1, at]
        dscores = (probs * (dprob_ref[:, at] - stat_ref[1:2, at])).astype(BF16)
        prob_ref[:, at] = probs.astype(BF16)
        dscore_ref[:, at] = dscores
        grad_query = dot(far_keys, far_dscore_ref[:, at], NN) + dot(near_keys, dscores, NN)
        grad_query = (grad_query * SCALE).T.astype(BF16)
        for h in range(PAIR):
            head = slice((step * PAIR + h) * HEAD_DIM, (step * PAIR + h + 1) * HEAD_DIM)
            grad_query_ref[:, head] = grad_query[h * TOK : (h + 1) * TOK]
        out_copy(step).start()
    keys = dot(dscore_ref[...], query_ref[...], NN) * SCALE
    values = dot(prob_ref[...], grad_ref[...], NN)
    for at, sums_ref in enumerate((one_sums_ref, three_sums_ref, own_sums_ref)):
        rows = slice(at * TOK, (at + 1) * TOK)
        sums_ref[:TOK] = keys[rows]
        sums_ref[TOK:] = values[rows]
    for step in range(STEPS):
        out_copy(step).wait()


WHOLE = pl.BlockSpec(memory_space=pltpu.VMEM)
SCALARS = pl.BlockSpec(memory_space=pltpu.SMEM)
FAR = pl.BlockSpec(memory_space=pl.ANY)


def call(kernel, name, flops, in_specs, outs, scratch, *args):
    return pl.pallas_call(
        kernel,
        out_shape=[jax.ShapeDtypeStruct(shape, dtype) for shape, dtype, _ in outs],
        in_specs=in_specs,
        out_specs=[spec for _, _, spec in outs],
        scratch_shapes=scratch,
        compiler_params=pltpu.CompilerParams(vmem_limit_bytes=16 * 1024 * 1024),
        cost_estimate=pl.CostEstimate(flops=flops, bytes_accessed=10**6, transcendentals=10**5),
        name=name,
    )(*args)


STACKED = ((ROWS, HEAD_DIM), BF16, WHOLE)
STATS = ((8, ROWS), F32, WHOLE)


def scores_of(blocks, dtype):
    return ((blocks * TOK, ROWS), dtype, WHOLE)


def load(*args):
    outs = [STACKED] * 2 + [((blocks * TOK, WIDE), F32, WHOLE) for blocks in (3, 2)]
    return call(load_kernel, "load", 2 * 10**8, [SCALARS] * 2 + [WHOLE] * 2, outs, [], *args)


def near_part(*args):
    return call(near_kernel, "near_part", 4 * 10**8, [WHOLE] * 6, [scores_of(3, F32)] * 2 + [STATS], [], *args)


def far_part(*args):
    outs = [((4 * TOK, HEAD_DIM), BF16, WHOLE), scores_of(2, BF16), STATS]
    scratch = [pltpu.VMEM((2 * TOK, ROWS), BF16)]
    return call(far_kernel, "far_part", 6 * 10**8, [WHOLE] * 6, outs, scratch, *args)


def rest_part(*args):
    outs = [((TOK, GROUP * HEAD_DIM), BF16, FAR)] + [((2 * TOK, HEAD_DIM), F32, WHOLE)] * 3
    scratch = [
        pltpu.VMEM((3 * TOK, ROWS), BF16),
        pltpu.VMEM((3 * TOK, ROWS), BF16),
        pltpu.VMEM((TOK, GROUP * HEAD_DIM), BF16),
        pltpu.SemaphoreType.DMA((STEPS,)),
    ]
    return call(rest_kernel, "rest_part", 8 * 10**8, [WHOLE] * 11, outs, scratch, *args)


def passed_along(array, by):
    devices = lax.axis_size("ctx")
    pairs = [(i, i + by) for i in range(devices) if 0 <= i + by < devices]
    return lax.ppermute(array, "ctx", pairs)


def local(queries, keys, values, grad_out, doc_lengths):
    index = lax.axis_index("ctx").astype(jnp.int32).reshape(1)
    low = jnp.array(-jnp.inf, BF16)
    own = lax.max(
        lax.pad(keys, low, ((0, TOK, 0), (0, 0, 0))), lax.pad(values, low, ((TOK, 0, 0), (0, 0, 0)))
    )
    three = passed_along(own, 3)
    one = passed_along(own, 1)
    query, grad, near_bias, far_bias = load(index, doc_lengths, queries, grad_out)
    one, three, far_bias = lax.optimization_barrier((one, three, far_bias))
    far = passed_along(jnp.concatenate([one, three], axis=0), 1)
    weight, dprob, near_stat = near_part(near_bias, query, grad, one, three, own)
    two, four = far[: 2 * TOK], far[2 * TOK :]
    far_sums, far_dscore, stat = far_part(far_bias, query, grad, near_stat, two, four)
    far_sums = passed_along(far_sums, -1)
    grad_q, one_sums, three_sums, own_sums = rest_part(
        query, grad, weight, dprob, stat, far_dscore, one, two, three, four, own
    )
    three_sums = (three_sums + far_sums[2 * TOK :].astype(F32)).astype(BF16)
    one_sums = (one_sums + far_sums[: 2 * TOK].astype(F32)).astype(BF16)
    three_sums = passed_along(three_sums, -3)
    one_sums = passed_along(one_sums, -1)
    sums = (own_sums + three_sums.astype(F32) + one_sums.astype(F32)).astype(BF16)
    return (grad_q, key_of(sums), value_of(sums))


def solution(mesh):
    placed = (P("ctx", "tp"), P("ctx", "tp"), P("ctx", "tp"), P("ctx", "tp"), P())
    return jax.shard_map(
        local,
        mesh=mesh,
        in_specs=placed,
        out_specs=(P("ctx", "tp"), P("ctx", "tp"), P("ctx", "tp")),
        check_vma=False,
    )
```

```python
import math

import jax
import jax.numpy as jnp
from jax import lax
from jax.experimental import pallas as pl
from jax.experimental.pallas import tpu as pltpu
from jax.sharding import PartitionSpec as P

HEADS = 128
KV_HEADS = 8
HEAD_DIM = 128
REACH = 4
TOK = 128
GROUP = HEADS // KV_HEADS
ROWS = GROUP * TOK
PAIR = 2
WIDE = PAIR * TOK
STEPS = GROUP // PAIR
DOCS = 32
SCALE = 1.0 / math.sqrt(HEAD_DIM)
SCALE_LOG2E = SCALE * math.log2(math.e)
MASKED = -1e30
F32 = jnp.float32
BF16 = jnp.bfloat16
NT = (((1,), (1,)), ((), ()))
NN = (((1,), (0,)), ((), ()))


def dot(a, b, dims):
    return lax.dot_general(a, b, dims, preferred_element_type=F32)


def key_of(block):
    return block[:TOK]


def value_of(block):
    return block[TOK:]


def columns(step):
    return slice(step * WIDE, (step + 1) * WIDE)


def doc_starts(lengths_ref, row):
    total = jnp.int32(0)
    starts = jnp.zeros_like(row)
    for doc in range(DOCS):
        total = total + lengths_ref[doc]
        starts = jnp.where(total <= row, total, starts)
    return starts


def positions(index_ref, lengths_ref):
    first = index_ref[0] * TOK
    query_pos = first + lax.broadcasted_iota(jnp.int32, (1, TOK), 1)
    starts = doc_starts(lengths_ref, query_pos)
    key_pos = first + lax.broadcasted_iota(jnp.int32, (TOK, TOK), 0)
    return key_pos, starts


def bias_of(key_pos, starts):
    bias = jnp.where(key_pos >= starts, 0.0, MASKED)
    return jnp.concatenate([bias] * PAIR, axis=1)


def top(x):
    return jnp.max(x, axis=0, keepdims=True)


def total(x):
    return jnp.sum(x, axis=0, keepdims=True)


def hold_kernel(block_ref, out_ref):
    out_ref[...] = block_ref[...]


def load_kernel(
    index_ref, lengths_ref, wide_query_ref, wide_grad_ref, query_ref, grad_ref, near_bias_ref, far_bias_ref
):
    key_pos, starts = positions(index_ref, lengths_ref)
    row = lax.broadcasted_iota(jnp.int32, (TOK, WIDE), 0)
    lane = lax.broadcasted_iota(jnp.int32, (TOK, WIDE), 1)
    for at, back in enumerate((2, 1, 3)):
        near_bias_ref[at * TOK : (at + 1) * TOK, :] = bias_of(key_pos - back * TOK, starts)
    near_bias_ref[3 * TOK :, :] = jnp.where(row <= lax.rem(lane, TOK), bias_of(key_pos, starts), MASKED)
    far_bias_ref[...] = bias_of(key_pos - 4 * TOK, starts)
    for head in range(GROUP):
        there, here = slice(head * HEAD_DIM, (head + 1) * HEAD_DIM), slice(head * TOK, (head + 1) * TOK)
        query_ref[here, :] = wide_query_ref[:, there]
        grad_ref[here, :] = wide_grad_ref[:, there]


def near_kernel(
    bias_ref, query_ref, grad_ref, two_ref, one_ref, three_ref, own_ref, weight_ref, dprob_ref, stat_ref
):
    blocks = (two_ref, one_ref, three_ref, own_ref)
    keys = jnp.concatenate([key_of(block) for block in blocks], axis=0)
    values = jnp.concatenate([value_of(block) for block in blocks], axis=0)
    for step in range(STEPS):
        at = columns(step)
        scores = dot(keys, query_ref[at, :], NT) * SCALE_LOG2E + bias_ref[...]
        dprobs = dot(values, grad_ref[at, :], NT)
        peak = top(scores)
        weights = jnp.exp2(scores - peak)
        weight_ref[:, at] = weights
        dprob_ref[:, at] = dprobs
        stat_ref[0:1, at] = peak
        stat_ref[1:2, at] = total(weights)
        stat_ref[2:3, at] = total(weights * dprobs)


def far_kernel(
    bias_ref,
    query_ref,
    grad_ref,
    near_weight_ref,
    near_dprob_ref,
    near_stat_ref,
    four_ref,
    sums_ref,
    dscore_ref,
    stat_ref,
    prob_ref,
):
    two, four = slice(0, TOK), slice(TOK, 2 * TOK)
    for step in range(STEPS):
        at = columns(step)
        scores = dot(key_of(four_ref), query_ref[at, :], NT) * SCALE_LOG2E + bias_ref[...]
        dprobs = dot(value_of(four_ref), grad_ref[at, :], NT)
        near_peak = near_stat_ref[0:1, at]
        peak = jnp.maximum(top(scores), near_peak)
        weights = jnp.exp2(scores - peak)
        near_factor = jnp.exp2(near_peak - peak)
        inverse = 1.0 / (total(weights) + near_stat_ref[1:2, at] * near_factor)
        delta = (total(weights * dprobs) + near_stat_ref[2:3, at] * near_factor) * inverse
        near_factor = near_factor * inverse
        stat_ref[0:1, at] = near_factor
        stat_ref[1:2, at] = delta
        probs = near_weight_ref[two, at] * near_factor
        prob_ref[two, at] = probs.astype(BF16)
        dscore_ref[two, at] = (probs * (near_dprob_ref[two, at] - delta)).astype(BF16)
        probs = weights * inverse
        prob_ref[four, at] = probs.astype(BF16)
        dscore_ref[four, at] = (probs * (dprobs - delta)).astype(BF16)
    keys = (dot(dscore_ref[...], query_ref[...], NN) * SCALE).astype(BF16)
    values = dot(prob_ref[...], grad_ref[...], NN).astype(BF16)
    for at, rows in enumerate((two, four)):
        sums_ref[2 * at * TOK : (2 * at + 1) * TOK] = keys[rows]
        sums_ref[(2 * at + 1) * TOK : (2 * at + 2) * TOK] = values[rows]


def rest_kernel(
    query_ref,
    grad_ref,
    weight_ref,
    dprob_ref,
    stat_ref,
    far_dscore_ref,
    one_ref,
    two_ref,
    three_ref,
    four_ref,
    own_ref,
    grad_query_hbm,
    one_sums_ref,
    three_sums_ref,
    own_sums_ref,
    prob_ref,
    dscore_ref,
    grad_query_ref,
    out_sems,
):
    far_keys = jnp.concatenate([key_of(two_ref), key_of(four_ref)], axis=0).T
    near_keys = jnp.concatenate([key_of(one_ref), key_of(three_ref), key_of(own_ref)], axis=0).T

    def out_copy(step):
        at = pl.ds(step * WIDE, WIDE)
        return pltpu.make_async_copy(grad_query_ref.at[:, at], grad_query_hbm.at[:, at], out_sems.at[step])

    for step in range(STEPS):
        at = columns(step)
        probs = weight_ref[TOK:, at] * stat_ref[0:1, at]
        dscores = (probs * (dprob_ref[TOK:, at] - stat_ref[1:2, at])).astype(BF16)
        prob_ref[:, at] = probs.astype(BF16)
        dscore_ref[:, at] = dscores
        grad_query = dot(far_keys, far_dscore_ref[:, at], NN) + dot(near_keys, dscores, NN)
        grad_query = (grad_query * SCALE).T.astype(BF16)
        for h in range(PAIR):
            head = slice((step * PAIR + h) * HEAD_DIM, (step * PAIR + h + 1) * HEAD_DIM)
            grad_query_ref[:, head] = grad_query[h * TOK : (h + 1) * TOK]
        out_copy(step).start()
    keys = dot(dscore_ref[...], query_ref[...], NN) * SCALE
    values = dot(prob_ref[...], grad_ref[...], NN)
    for at, sums_ref in enumerate((one_sums_ref, three_sums_ref, own_sums_ref)):
        rows = slice(at * TOK, (at + 1) * TOK)
        sums_ref[:TOK] = keys[rows]
        sums_ref[TOK:] = values[rows]
    for step in range(STEPS):
        out_copy(step).wait()


WHOLE = pl.BlockSpec(memory_space=pltpu.VMEM)
SCALARS = pl.BlockSpec(memory_space=pltpu.SMEM)
FAR = pl.BlockSpec(memory_space=pl.ANY)


def call(kernel, name, flops, in_specs, outs, scratch, *args):
    return pl.pallas_call(
        kernel,
        out_shape=[jax.ShapeDtypeStruct(shape, dtype) for shape, dtype, _ in outs],
        in_specs=in_specs,
        out_specs=[spec for _, _, spec in outs],
        scratch_shapes=scratch,
        compiler_params=pltpu.CompilerParams(vmem_limit_bytes=16 * 1024 * 1024),
        cost_estimate=pl.CostEstimate(flops=flops, bytes_accessed=10**6, transcendentals=10**5),
        name=name,
    )(*args)


STACKED = ((ROWS, HEAD_DIM), BF16, WHOLE)
STATS = ((8, ROWS), F32, WHOLE)


def scores_of(blocks, dtype):
    return ((blocks * TOK, ROWS), dtype, WHOLE)


def hold(block):
    return call(hold_kernel, "hold_part", 10**10, [WHOLE], [((2 * TOK, HEAD_DIM), BF16, WHOLE)], [], block)[0]


def load(*args):
    outs = [STACKED] * 2 + [((blocks * TOK, WIDE), F32, WHOLE) for blocks in (4, 1)]
    return call(load_kernel, "load", 2 * 10**8, [SCALARS] * 2 + [WHOLE] * 2, outs, [], *args)


def near_part(*args):
    return call(near_kernel, "near_part", 5 * 10**8, [WHOLE] * 7, [scores_of(4, F32)] * 2 + [STATS], [], *args)


def far_part(*args):
    outs = [((4 * TOK, HEAD_DIM), BF16, WHOLE), scores_of(2, BF16), STATS]
    scratch = [pltpu.VMEM((2 * TOK, ROWS), BF16)]
    return call(far_kernel, "far_part", 6 * 10**8, [WHOLE] * 7, outs, scratch, *args)


def rest_part(*args):
    outs = [((TOK, GROUP * HEAD_DIM), BF16, FAR)] + [((2 * TOK, HEAD_DIM), F32, WHOLE)] * 3
    scratch = [
        pltpu.VMEM((3 * TOK, ROWS), BF16),
        pltpu.VMEM((3 * TOK, ROWS), BF16),
        pltpu.VMEM((TOK, GROUP * HEAD_DIM), BF16),
        pltpu.SemaphoreType.DMA((STEPS,)),
    ]
    return call(rest_kernel, "rest_part", 8 * 10**8, [WHOLE] * 11, outs, scratch, *args)


def passed_along(array, by):
    devices = lax.axis_size("ctx")
    pairs = [(i, i + by) for i in range(devices) if 0 <= i + by < devices]
    return lax.ppermute(array, "ctx", pairs)


def local(queries, keys, values, grad_out, doc_lengths):
    index = lax.axis_index("ctx").astype(jnp.int32).reshape(1)
    low = jnp.array(-jnp.inf, BF16)
    own = lax.max(
        lax.pad(keys, low, ((0, TOK, 0), (0, 0, 0))), lax.pad(values, low, ((TOK, 0, 0), (0, 0, 0)))
    )
    own = hold(own)
    three = passed_along(own, 3)
    one = passed_along(own, 1)
    two = passed_along(own, 2)
    query, grad, near_bias, far_bias = load(index, doc_lengths, queries, grad_out)
    four = passed_along(three, 1)
    weight, dprob, near_stat = near_part(near_bias, query, grad, two, one, three, own)
    far_sums, far_dscore, stat = far_part(far_bias, query, grad, weight, dprob, near_stat, four)
    far_sums = passed_along(far_sums, -1)
    grad_q, one_sums, three_sums, own_sums = rest_part(
        query, grad, weight, dprob, stat, far_dscore, one, two, three, four, own
    )
    three_sums = (three_sums + far_sums[2 * TOK :].astype(F32)).astype(BF16)
    one_sums = (one_sums + far_sums[: 2 * TOK].astype(F32)).astype(BF16)
    three_sums = passed_along(three_sums, -3)
    one_sums = passed_along(one_sums, -1)
    sums = (own_sums + three_sums.astype(F32) + one_sums.astype(F32)).astype(BF16)
    return (grad_q, key_of(sums), value_of(sums))


def solution(mesh):
    placed = (P("ctx", "tp"), P("ctx", "tp"), P("ctx", "tp"), P("ctx", "tp"), P())
    return jax.shard_map(
        local,
        mesh=mesh,
        in_specs=placed,
        out_specs=(P("ctx", "tp"), P("ctx", "tp"), P("ctx", "tp")),
        check_vma=False,
    )
```

```python
import math

import jax
import jax.numpy as jnp
from jax import lax
from jax.experimental import pallas as pl
from jax.experimental.pallas import tpu as pltpu
from jax.sharding import PartitionSpec as P

HEADS = 128
KV_HEADS = 8
HEAD_DIM = 128
REACH = 4
TOK = 128
GROUP = HEADS // KV_HEADS
ROWS = GROUP * TOK
PAIR = 2
WIDE = PAIR * TOK
STEPS = GROUP // PAIR
DOCS = 32
SCALE = 1.0 / math.sqrt(HEAD_DIM)
SCALE_LOG2E = SCALE * math.log2(math.e)
MASKED = -1e30
F32 = jnp.float32
BF16 = jnp.bfloat16
NT = (((1,), (1,)), ((), ()))
NN = (((1,), (0,)), ((), ()))


def dot(a, b, dims):
    return lax.dot_general(a, b, dims, preferred_element_type=F32)


def key_of(block):
    return block[:TOK]


def value_of(block):
    return block[TOK:]


def columns(step):
    return slice(step * WIDE, (step + 1) * WIDE)


def doc_starts(lengths_ref, row):
    total = jnp.int32(0)
    starts = jnp.zeros_like(row)
    for doc in range(DOCS):
        total = total + lengths_ref[doc]
        starts = jnp.where(total <= row, total, starts)
    return starts


def positions(index_ref, lengths_ref):
    first = index_ref[0] * TOK
    query_pos = first + lax.broadcasted_iota(jnp.int32, (1, TOK), 1)
    starts = doc_starts(lengths_ref, query_pos)
    key_pos = first + lax.broadcasted_iota(jnp.int32, (TOK, TOK), 0)
    return key_pos, starts


def bias_of(key_pos, starts):
    bias = jnp.where(key_pos >= starts, 0.0, MASKED)
    return jnp.concatenate([bias] * PAIR, axis=1)


def top(x):
    return jnp.max(x, axis=0, keepdims=True)


def total(x):
    return jnp.sum(x, axis=0, keepdims=True)


def hold_kernel(block_ref, out_ref):
    out_ref[...] = block_ref[...]


def load_kernel(
    index_ref, lengths_ref, wide_query_ref, wide_grad_ref, query_ref, grad_ref, near_bias_ref, far_bias_ref
):
    key_pos, starts = positions(index_ref, lengths_ref)
    row = lax.broadcasted_iota(jnp.int32, (TOK, WIDE), 0)
    lane = lax.broadcasted_iota(jnp.int32, (TOK, WIDE), 1)
    for at, back in enumerate((2, 1, 3)):
        near_bias_ref[at * TOK : (at + 1) * TOK, :] = bias_of(key_pos - back * TOK, starts)
    near_bias_ref[3 * TOK :, :] = jnp.where(row <= lax.rem(lane, TOK), bias_of(key_pos, starts), MASKED)
    far_bias_ref[...] = bias_of(key_pos - 4 * TOK, starts)
    for head in range(GROUP):
        there, here = slice(head * HEAD_DIM, (head + 1) * HEAD_DIM), slice(head * TOK, (head + 1) * TOK)
        query_ref[here, :] = wide_query_ref[:, there]
        grad_ref[here, :] = wide_grad_ref[:, there]


def near_kernel(
    bias_ref, query_ref, grad_ref, one_ref, two_ref, three_ref, own_ref, weight_ref, dprob_ref, stat_ref
):
    blocks = (two_ref, one_ref, three_ref, own_ref)
    keys = jnp.concatenate([key_of(block) for block in blocks], axis=0)
    values = jnp.concatenate([value_of(block) for block in blocks], axis=0)
    for step in range(STEPS):
        at = columns(step)
        scores = dot(keys, query_ref[at, :], NT) * SCALE_LOG2E + bias_ref[...]
        dprobs = dot(values, grad_ref[at, :], NT)
        peak = top(scores)
        weights = jnp.exp2(scores - peak)
        weight_ref[:, at] = weights
        dprob_ref[:, at] = dprobs
        stat_ref[0:1, at] = peak
        stat_ref[1:2, at] = total(weights)
        stat_ref[2:3, at] = total(weights * dprobs)


def far_kernel(
    bias_ref,
    query_ref,
    grad_ref,
    near_weight_ref,
    near_dprob_ref,
    near_stat_ref,
    four_ref,
    sums_ref,
    dscore_ref,
    stat_ref,
    prob_ref,
):
    two, four = slice(0, TOK), slice(TOK, 2 * TOK)
    for step in range(STEPS):
        at = columns(step)
        scores = dot(key_of(four_ref), query_ref[at, :], NT) * SCALE_LOG2E + bias_ref[...]
        dprobs = dot(value_of(four_ref), grad_ref[at, :], NT)
        near_peak = near_stat_ref[0:1, at]
        peak = jnp.maximum(top(scores), near_peak)
        weights = jnp.exp2(scores - peak)
        near_factor = jnp.exp2(near_peak - peak)
        inverse = 1.0 / (total(weights) + near_stat_ref[1:2, at] * near_factor)
        delta = (total(weights * dprobs) + near_stat_ref[2:3, at] * near_factor) * inverse
        near_factor = near_factor * inverse
        stat_ref[0:1, at] = near_factor
        stat_ref[1:2, at] = delta
        probs = near_weight_ref[two, at] * near_factor
        prob_ref[two, at] = probs.astype(BF16)
        dscore_ref[two, at] = (probs * (near_dprob_ref[two, at] - delta)).astype(BF16)
        probs = weights * inverse
        prob_ref[four, at] = probs.astype(BF16)
        dscore_ref[four, at] = (probs * (dprobs - delta)).astype(BF16)
    keys = (dot(dscore_ref[...], query_ref[...], NN) * SCALE).astype(BF16)
    values = dot(prob_ref[...], grad_ref[...], NN).astype(BF16)
    for at, rows in enumerate((two, four)):
        sums_ref[2 * at * TOK : (2 * at + 1) * TOK] = keys[rows]
        sums_ref[(2 * at + 1) * TOK : (2 * at + 2) * TOK] = values[rows]


def rest_kernel(
    query_ref,
    grad_ref,
    weight_ref,
    dprob_ref,
    stat_ref,
    far_dscore_ref,
    one_ref,
    two_ref,
    three_ref,
    four_ref,
    own_ref,
    grad_query_hbm,
    one_sums_ref,
    three_sums_ref,
    own_sums_ref,
    prob_ref,
    dscore_ref,
    grad_query_ref,
    out_sems,
):
    far_keys = jnp.concatenate([key_of(two_ref), key_of(four_ref)], axis=0).T
    near_keys = jnp.concatenate([key_of(one_ref), key_of(three_ref), key_of(own_ref)], axis=0).T

    def out_copy(step):
        at = pl.ds(step * WIDE, WIDE)
        return pltpu.make_async_copy(grad_query_ref.at[:, at], grad_query_hbm.at[:, at], out_sems.at[step])

    for step in range(STEPS):
        at = columns(step)
        probs = weight_ref[TOK:, at] * stat_ref[0:1, at]
        dscores = (probs * (dprob_ref[TOK:, at] - stat_ref[1:2, at])).astype(BF16)
        prob_ref[:, at] = probs.astype(BF16)
        dscore_ref[:, at] = dscores
        grad_query = dot(far_keys, far_dscore_ref[:, at], NN) + dot(near_keys, dscores, NN)
        grad_query = (grad_query * SCALE).T.astype(BF16)
        for h in range(PAIR):
            head = slice((step * PAIR + h) * HEAD_DIM, (step * PAIR + h + 1) * HEAD_DIM)
            grad_query_ref[:, head] = grad_query[h * TOK : (h + 1) * TOK]
        out_copy(step).start()
    keys = dot(dscore_ref[...], query_ref[...], NN) * SCALE
    values = dot(prob_ref[...], grad_ref[...], NN)
    for at, sums_ref in enumerate((one_sums_ref, three_sums_ref, own_sums_ref)):
        rows = slice(at * TOK, (at + 1) * TOK)
        sums_ref[:TOK] = keys[rows]
        sums_ref[TOK:] = values[rows]
    for step in range(STEPS):
        out_copy(step).wait()


WHOLE = pl.BlockSpec(memory_space=pltpu.VMEM)
SCALARS = pl.BlockSpec(memory_space=pltpu.SMEM)
FAR = pl.BlockSpec(memory_space=pl.ANY)


def call(kernel, name, flops, in_specs, outs, scratch, *args):
    return pl.pallas_call(
        kernel,
        out_shape=[jax.ShapeDtypeStruct(shape, dtype) for shape, dtype, _ in outs],
        in_specs=in_specs,
        out_specs=[spec for _, _, spec in outs],
        scratch_shapes=scratch,
        compiler_params=pltpu.CompilerParams(vmem_limit_bytes=16 * 1024 * 1024),
        cost_estimate=pl.CostEstimate(flops=flops, bytes_accessed=10**6, transcendentals=10**5),
        name=name,
    )(*args)


STACKED = ((ROWS, HEAD_DIM), BF16, WHOLE)
STATS = ((8, ROWS), F32, WHOLE)


def scores_of(blocks, dtype):
    return ((blocks * TOK, ROWS), dtype, WHOLE)


def hold(block):
    return call(hold_kernel, "hold_part", 10**10, [WHOLE], [((2 * TOK, HEAD_DIM), BF16, WHOLE)], [], block)[0]


def load(*args):
    outs = [STACKED] * 2 + [((blocks * TOK, WIDE), F32, WHOLE) for blocks in (4, 1)]
    return call(load_kernel, "load", 2 * 10**8, [SCALARS] * 2 + [WHOLE] * 2, outs, [], *args)


def near_part(*args):
    return call(near_kernel, "near_part", 5 * 10**8, [WHOLE] * 7, [scores_of(4, F32)] * 2 + [STATS], [], *args)


def far_part(*args):
    outs = [((4 * TOK, HEAD_DIM), BF16, WHOLE), scores_of(2, BF16), STATS]
    scratch = [pltpu.VMEM((2 * TOK, ROWS), BF16)]
    return call(far_kernel, "far_part", 6 * 10**8, [WHOLE] * 7, outs, scratch, *args)


def rest_part(*args):
    outs = [((TOK, GROUP * HEAD_DIM), BF16, FAR)] + [((2 * TOK, HEAD_DIM), F32, WHOLE)] * 3
    scratch = [
        pltpu.VMEM((3 * TOK, ROWS), BF16),
        pltpu.VMEM((3 * TOK, ROWS), BF16),
        pltpu.VMEM((TOK, GROUP * HEAD_DIM), BF16),
        pltpu.SemaphoreType.DMA((STEPS,)),
    ]
    return call(rest_kernel, "rest_part", 8 * 10**8, [WHOLE] * 11, outs, scratch, *args)


def passed_along(array, by):
    devices = lax.axis_size("ctx")
    pairs = [(i, i + by) for i in range(devices) if 0 <= i + by < devices]
    return lax.ppermute(array, "ctx", pairs)


def local(queries, keys, values, grad_out, doc_lengths):
    index = lax.axis_index("ctx").astype(jnp.int32).reshape(1)
    low = jnp.array(-jnp.inf, BF16)
    own = lax.max(
        lax.pad(keys, low, ((0, TOK, 0), (0, 0, 0))), lax.pad(values, low, ((TOK, 0, 0), (0, 0, 0)))
    )
    own = hold(own)
    three = passed_along(own, 3)
    one = passed_along(own, 1)
    two = passed_along(own, 2)
    query, grad, near_bias, far_bias = load(index, doc_lengths, queries, grad_out)
    four = passed_along(three, 1)
    weight, dprob, near_stat = near_part(near_bias, query, grad, one, two, three, own)
    far_sums, far_dscore, stat = far_part(far_bias, query, grad, weight, dprob, near_stat, four)
    far_sums = passed_along(far_sums, -1)
    grad_q, one_sums, three_sums, own_sums = rest_part(
        query, grad, weight, dprob, stat, far_dscore, one, two, three, four, own
    )
    three_sums = (three_sums + far_sums[2 * TOK :].astype(F32)).astype(BF16)
    one_sums = (one_sums + far_sums[: 2 * TOK].astype(F32)).astype(BF16)
    three_sums = passed_along(three_sums, -3)
    one_sums = passed_along(one_sums, -1)
    sums = (own_sums + three_sums.astype(F32) + one_sums.astype(F32)).astype(BF16)
    return (grad_q, key_of(sums), value_of(sums))


def solution(mesh):
    placed = (P("ctx", "tp"), P("ctx", "tp"), P("ctx", "tp"), P("ctx", "tp"), P())
    return jax.shard_map(
        local,
        mesh=mesh,
        in_specs=placed,
        out_specs=(P("ctx", "tp"), P("ctx", "tp"), P("ctx", "tp")),
        check_vma=False,
    )
```

```python
import math

import jax
import jax.numpy as jnp
from jax import lax
from jax.experimental import pallas as pl
from jax.experimental.pallas import tpu as pltpu
from jax.sharding import PartitionSpec as P

HEADS = 128
KV_HEADS = 8
HEAD_DIM = 128
REACH = 4
TOK = 128
GROUP = HEADS // KV_HEADS
ROWS = GROUP * TOK
PAIR = 2
WIDE = PAIR * TOK
STEPS = GROUP // PAIR
DOCS = 32
SCALE = 1.0 / math.sqrt(HEAD_DIM)
SCALE_LOG2E = SCALE * math.log2(math.e)
MASKED = -1e30
F32 = jnp.float32
BF16 = jnp.bfloat16
NT = (((1,), (1,)), ((), ()))
NN = (((1,), (0,)), ((), ()))


def dot(a, b, dims):
    return lax.dot_general(a, b, dims, preferred_element_type=F32)


def key_of(block):
    return block[:TOK]


def value_of(block):
    return block[TOK:]


def columns(step):
    return slice(step * WIDE, (step + 1) * WIDE)


def doc_starts(lengths_ref, row):
    total = jnp.int32(0)
    starts = jnp.zeros_like(row)
    for doc in range(DOCS):
        total = total + lengths_ref[doc]
        starts = jnp.where(total <= row, total, starts)
    return starts


def positions(index_ref, lengths_ref):
    first = index_ref[0] * TOK
    query_pos = first + lax.broadcasted_iota(jnp.int32, (1, TOK), 1)
    starts = doc_starts(lengths_ref, query_pos)
    key_pos = first + lax.broadcasted_iota(jnp.int32, (TOK, TOK), 0)
    return key_pos, starts


def bias_of(key_pos, starts):
    bias = jnp.where(key_pos >= starts, 0.0, MASKED)
    return jnp.concatenate([bias] * PAIR, axis=1)


def top(x):
    return jnp.max(x, axis=0, keepdims=True)


def total(x):
    return jnp.sum(x, axis=0, keepdims=True)


def hold_kernel(block_ref, out_ref):
    out_ref[...] = block_ref[...]


def load_kernel(
    index_ref, lengths_ref, wide_query_ref, wide_grad_ref, query_ref, grad_ref, near_bias_ref, far_bias_ref
):
    key_pos, starts = positions(index_ref, lengths_ref)
    row = lax.broadcasted_iota(jnp.int32, (TOK, WIDE), 0)
    lane = lax.broadcasted_iota(jnp.int32, (TOK, WIDE), 1)
    for at, back in enumerate((2, 1, 3)):
        near_bias_ref[at * TOK : (at + 1) * TOK, :] = bias_of(key_pos - back * TOK, starts)
    near_bias_ref[3 * TOK :, :] = jnp.where(row <= lax.rem(lane, TOK), bias_of(key_pos, starts), MASKED)
    far_bias_ref[...] = bias_of(key_pos - 4 * TOK, starts)
    for head in range(GROUP):
        there, here = slice(head * HEAD_DIM, (head + 1) * HEAD_DIM), slice(head * TOK, (head + 1) * TOK)
        query_ref[here, :] = wide_query_ref[:, there]
        grad_ref[here, :] = wide_grad_ref[:, there]


def near_kernel(
    bias_ref, query_ref, grad_ref, two_ref, one_ref, three_ref, own_ref, weight_ref, dprob_ref, stat_ref
):
    blocks = (two_ref, one_ref, three_ref, own_ref)
    keys = jnp.concatenate([key_of(block) for block in blocks], axis=0)
    values = jnp.concatenate([value_of(block) for block in blocks], axis=0)
    for step in range(STEPS):
        at = columns(step)
        scores = dot(keys, query_ref[at, :], NT) * SCALE_LOG2E + bias_ref[...]
        dprobs = dot(values, grad_ref[at, :], NT)
        peak = top(scores)
        weights = jnp.exp2(scores - peak)
        weight_ref[:, at] = weights
        dprob_ref[:, at] = dprobs
        stat_ref[0:1, at] = peak
        stat_ref[1:2, at] = total(weights)
        stat_ref[2:3, at] = total(weights * dprobs)


def far_kernel(
    bias_ref,
    query_ref,
    grad_ref,
    near_weight_ref,
    near_dprob_ref,
    near_stat_ref,
    four_ref,
    sums_ref,
    dscore_ref,
    stat_ref,
    prob_ref,
):
    two, four = slice(0, TOK), slice(TOK, 2 * TOK)
    for step in range(STEPS):
        at = columns(step)
        scores = dot(key_of(four_ref), query_ref[at, :], NT) * SCALE_LOG2E + bias_ref[...]
        dprobs = dot(value_of(four_ref), grad_ref[at, :], NT)
        near_peak = near_stat_ref[0:1, at]
        peak = jnp.maximum(top(scores), near_peak)
        weights = jnp.exp2(scores - peak)
        near_factor = jnp.exp2(near_peak - peak)
        inverse = 1.0 / (total(weights) + near_stat_ref[1:2, at] * near_factor)
        delta = (total(weights * dprobs) + near_stat_ref[2:3, at] * near_factor) * inverse
        near_factor = near_factor * inverse
        stat_ref[0:1, at] = near_factor
        stat_ref[1:2, at] = delta
        probs = near_weight_ref[two, at] * near_factor
        prob_ref[two, at] = probs.astype(BF16)
        dscore_ref[two, at] = (probs * (near_dprob_ref[two, at] - delta)).astype(BF16)
        probs = weights * inverse
        prob_ref[four, at] = probs.astype(BF16)
        dscore_ref[four, at] = (probs * (dprobs - delta)).astype(BF16)
    keys = (dot(dscore_ref[...], query_ref[...], NN) * SCALE).astype(BF16)
    values = dot(prob_ref[...], grad_ref[...], NN).astype(BF16)
    for at, rows in enumerate((two, four)):
        sums_ref[2 * at * TOK : (2 * at + 1) * TOK] = keys[rows]
        sums_ref[(2 * at + 1) * TOK : (2 * at + 2) * TOK] = values[rows]


def rest_kernel(
    query_ref,
    grad_ref,
    weight_ref,
    dprob_ref,
    stat_ref,
    far_dscore_ref,
    one_ref,
    two_ref,
    three_ref,
    four_ref,
    own_ref,
    grad_query_hbm,
    one_sums_ref,
    three_sums_ref,
    own_sums_ref,
    prob_ref,
    dscore_ref,
    grad_query_ref,
    out_sems,
):
    far_keys = jnp.concatenate([key_of(two_ref), key_of(four_ref)], axis=0).T
    near_keys = jnp.concatenate([key_of(one_ref), key_of(three_ref), key_of(own_ref)], axis=0).T

    def out_copy(step):
        at = pl.ds(step * WIDE, WIDE)
        return pltpu.make_async_copy(grad_query_ref.at[:, at], grad_query_hbm.at[:, at], out_sems.at[step])

    for step in range(STEPS):
        at = columns(step)
        probs = weight_ref[TOK:, at] * stat_ref[0:1, at]
        dscores = (probs * (dprob_ref[TOK:, at] - stat_ref[1:2, at])).astype(BF16)
        prob_ref[:, at] = probs.astype(BF16)
        dscore_ref[:, at] = dscores
        grad_query = dot(far_keys, far_dscore_ref[:, at], NN) + dot(near_keys, dscores, NN)
        grad_query = (grad_query * SCALE).T.astype(BF16)
        for h in range(PAIR):
            head = slice((step * PAIR + h) * HEAD_DIM, (step * PAIR + h + 1) * HEAD_DIM)
            grad_query_ref[:, head] = grad_query[h * TOK : (h + 1) * TOK]
        out_copy(step).start()
    keys = dot(dscore_ref[...], query_ref[...], NN) * SCALE
    values = dot(prob_ref[...], grad_ref[...], NN)
    for at, sums_ref in enumerate((one_sums_ref, three_sums_ref, own_sums_ref)):
        rows = slice(at * TOK, (at + 1) * TOK)
        sums_ref[:TOK] = keys[rows]
        sums_ref[TOK:] = values[rows]
    for step in range(STEPS):
        out_copy(step).wait()


WHOLE = pl.BlockSpec(memory_space=pltpu.VMEM)
SCALARS = pl.BlockSpec(memory_space=pltpu.SMEM)
FAR = pl.BlockSpec(memory_space=pl.ANY)


def call(kernel, name, flops, in_specs, outs, scratch, *args):
    return pl.pallas_call(
        kernel,
        out_shape=[jax.ShapeDtypeStruct(shape, dtype) for shape, dtype, _ in outs],
        in_specs=in_specs,
        out_specs=[spec for _, _, spec in outs],
        scratch_shapes=scratch,
        compiler_params=pltpu.CompilerParams(vmem_limit_bytes=16 * 1024 * 1024),
        cost_estimate=pl.CostEstimate(flops=flops, bytes_accessed=10**6, transcendentals=10**5),
        name=name,
    )(*args)


STACKED = ((ROWS, HEAD_DIM), BF16, WHOLE)
STATS = ((8, ROWS), F32, WHOLE)


def scores_of(blocks, dtype):
    return ((blocks * TOK, ROWS), dtype, WHOLE)


def hold(block):
    return call(hold_kernel, "hold_part", 10**10, [WHOLE], [((2 * TOK, HEAD_DIM), BF16, WHOLE)], [], block)[0]


def load(*args):
    outs = [STACKED] * 2 + [((blocks * TOK, WIDE), F32, WHOLE) for blocks in (4, 1)]
    return call(load_kernel, "load", 2 * 10**8, [SCALARS] * 2 + [WHOLE] * 2, outs, [], *args)


def near_part(*args):
    return call(near_kernel, "near_part", 5 * 10**8, [WHOLE] * 7, [scores_of(4, F32)] * 2 + [STATS], [], *args)


def far_part(*args):
    outs = [((4 * TOK, HEAD_DIM), BF16, WHOLE), scores_of(2, BF16), STATS]
    scratch = [pltpu.VMEM((2 * TOK, ROWS), BF16)]
    return call(far_kernel, "far_part", 6 * 10**8, [WHOLE] * 7, outs, scratch, *args)


def rest_part(*args):
    outs = [((TOK, GROUP * HEAD_DIM), BF16, FAR)] + [((2 * TOK, HEAD_DIM), F32, WHOLE)] * 3
    scratch = [
        pltpu.VMEM((3 * TOK, ROWS), BF16),
        pltpu.VMEM((3 * TOK, ROWS), BF16),
        pltpu.VMEM((TOK, GROUP * HEAD_DIM), BF16),
        pltpu.SemaphoreType.DMA((STEPS,)),
    ]
    return call(rest_kernel, "rest_part", 8 * 10**8, [WHOLE] * 11, outs, scratch, *args)


def passed_along(array, by):
    devices = lax.axis_size("ctx")
    pairs = [(i, i + by) for i in range(devices) if 0 <= i + by < devices]
    return lax.ppermute(array, "ctx", pairs)


def local(queries, keys, values, grad_out, doc_lengths):
    index = lax.axis_index("ctx").astype(jnp.int32).reshape(1)
    low = jnp.array(-jnp.inf, BF16)
    own = lax.max(
        lax.pad(keys, low, ((0, TOK, 0), (0, 0, 0))), lax.pad(values, low, ((TOK, 0, 0), (0, 0, 0)))
    )
    own = hold(own)
    three = passed_along(own, 3)
    one = passed_along(own, 1)
    two = passed_along(own, 2)
    query, grad, near_bias, far_bias = load(index, doc_lengths, queries, grad_out)
    four = passed_along(three, 1)
    weight, dprob, near_stat = near_part(near_bias, query, grad, two, one, three, own)
    far_sums, far_dscore, stat = far_part(far_bias, query, grad, weight, dprob, near_stat, four)
    far_sums = passed_along(far_sums, -1)
    grad_q, one_sums, three_sums, own_sums = rest_part(
        query, grad, weight, dprob, stat, far_dscore, one, two, three, four, own
    )
    three_sums = (three_sums + far_sums[2 * TOK :].astype(F32)).astype(BF16)
    one_sums = (one_sums + far_sums[: 2 * TOK].astype(F32)).astype(BF16)
    three_sums = passed_along(three_sums, -3)
    one_sums = passed_along(one_sums, -1)
    parts = (own_sums, three_sums.astype(F32), one_sums.astype(F32))
    grad_k, grad_v = [(of(parts[0]) + of(parts[1]) + of(parts[2])).astype(BF16) for of in (key_of, value_of)]
    return (grad_q, grad_k, grad_v)


def solution(mesh):
    placed = (P("ctx", "tp"), P("ctx", "tp"), P("ctx", "tp"), P("ctx", "tp"), P())
    return jax.shard_map(
        local,
        mesh=mesh,
        in_specs=placed,
        out_specs=(P("ctx", "tp"), P("ctx", "tp"), P("ctx", "tp")),
        check_vma=False,
    )
```
